32 devices in a mesh: seq: 8 (over z, y), head: 4 (over x, core).
Axes of the slice: x: 2, y: 2, z: 4, core: 2. Of those that a mesh axis runs over, the one named last changes fastest.
Arguments:
- queries: bfloat16 [1024, 4096], P('seq', 'head')
- keys: bfloat16 [1024, 1024], P('seq', 'head')
- values: bfloat16 [1024, 1024], P('seq', 'head'), may hold values from -6 to 6
- out_weight: bfloat16 [4096, 4096], P('head'), may hold values from -0.09375 to 0.09375
- windows: int32 [32], replicated, may hold values from 128 to 512, as said below
- seg_lengths: int32 [64], replicated, may hold values from 1 to 48, 1024 in all
- lang_ids: int32 [64], replicated, may hold values from 0 to 7
Outputs:
- centered: bfloat16 [1024, 4096], P('seq', 'head')
- pooled: float32 [64, 4096], P(None, 'head')
The draws below stay inside these ranges and needn't reach their ends.
Inputs may be any that keep to these rules, and one draw needn't show every extreme that they name: `windows`: each head's window; some head has exactly 512. `seg_lengths`: the spans tile the document; the longest is exactly 48.
All inputs are finite; a program needn't handle non-finite values.
Results may differ from the reference program's by a relative error of at most 0.014.
Values may be sent and summed in bfloat16 or wider, within the bound.
A program may use at most 64 MiB of HBM per device.

```python
import math
import jax
import jax.numpy as jnp
import numpy as np
from jax import lax

D = 4096
HEADS = 32
KVH = 8
HD = 128
TOK_DEV = 128
SEGS = 64
NLANG = 8
WINDOW = 512
LENGTH = 1024
SEG_MOST = 48
N_SEQ = 8


def draw_keys(key, part):
    base = jax.random.normal(jax.random.fold_in(key, 11), (LENGTH, KVH * HD), jnp.float32)
    return base.astype(jnp.bfloat16)


def draw_queries(key, part):
    found = 2.5 * jax.random.normal(jax.random.fold_in(key, 21), (LENGTH, HEADS, HD), jnp.float32)
    return found.reshape(LENGTH, HEADS * HD).astype(jnp.bfloat16)


def draw_windows(key, part):
    spread = jax.random.randint(jax.random.fold_in(key, 31), (HEADS,), WINDOW // 4, WINDOW + 1)
    widest = jax.random.randint(jax.random.fold_in(key, 32), (), 0, HEADS)
    return jnp.where(jnp.arange(HEADS) == widest, WINDOW, spread).astype(jnp.int32)


def set_ends(entries, key, smallest, high):
    shape = entries.shape
    place = [jax.random.randint(jax.random.fold_in(key, axis), (), 0, shape[axis]) for axis in range(len(shape))]
    entries = entries.at[tuple(place)].set(smallest)
    longest = shape.index(max(shape))
    place[longest] = (place[longest] + 1) % shape[longest]
    return entries.at[tuple(place)].set(high)


def shard_levels(own_key, extent, pieces, least, top_value):
    factor_of = 1.0
    for axis_at, parts in pieces:
        heights = jax.random.uniform(jax.random.fold_in(jax.random.fold_in(own_key, 6), axis_at), (parts,), jnp.float32, least / len(pieces), top_value / len(pieces))
        factor_of = factor_of * jnp.repeat(jnp.exp(heights), extent[axis_at] // parts).reshape((-1,) + (1,) * (len(extent) - 1 - axis_at))
    return factor_of


def length_profile(amount, total, bound, skew):
    portions = [(1 << 20) // math.isqrt(standing ** skew) + 1 for standing in range(2, amount + 1)]
    spare, counts = total - bound - (amount - 1), [1] * (amount - 1)
    while spare > 0:
        movable = [i for i in range(amount - 1) if counts[i] < bound]
        whole, remaining = sum([portions[i] for i in movable]), spare
        for i in movable:
            more = min(bound - counts[i], max(1, remaining * portions[i] // whole), spare)
            counts[i] = counts[i] + more
            spare = spare - more
    return np.array([bound] + counts)


def ragged(stream_key, count, total, bound, lean):
    if count == 2:
        one = jax.random.randint(stream_key, (), max(1, total - bound), min(bound, total - 1) + 1)
        return jnp.stack([one, total - one])
    sizes = jnp.asarray(length_profile(count, total, bound, lean), jnp.int32)
    pairs = (count - 1) // 2
    source_of, receiver = sizes[1:1 + 2 * pairs:2], sizes[2:2 + 2 * pairs:2]
    room = jnp.minimum(source_of - 1, bound - receiver)
    shifted = jax.random.randint(jax.random.fold_in(stream_key, 1), (pairs,), 0, 1 << 20) % (room + 1)
    sizes = sizes.at[1:1 + 2 * pairs:2].set(source_of - shifted).at[2:2 + 2 * pairs:2].set(receiver + shifted)
    return sizes[jax.random.permutation(jax.random.fold_in(stream_key, 2), count)]


def scatter_about(stream_key, extent, scale, reach, shards=(), kind=jnp.bfloat16):
    level = shard_levels(stream_key, extent, shards, -0.22, 0.18) if shards else 1.0
    drawn = jax.random.normal(stream_key, extent, jnp.float32) * scale * level
    return jnp.minimum(jnp.maximum(drawn, -reach), reach).astype(kind)


def setup_inputs(seed: int = 0) -> dict:
    key_of = jax.random.split(jax.random.key(seed), 8)
    queries = draw_queries(jax.random.fold_in(key_of[7], 71), 0)
    keys = draw_keys(jax.random.fold_in(key_of[7], 71), 0)
    values = scatter_about(key_of[2], (LENGTH, KVH * HD), 1.0, 6.0, ((0, 8), (1, 4)))
    out_weight = scatter_about(key_of[3], (HEADS * HD, D), (HEADS * HD) ** -0.5, 0.09375, ((0, 4),))
    windows = draw_windows(jax.random.fold_in(key_of[7], 71), 0)
    seg_lengths = ragged(key_of[5], SEGS, LENGTH, SEG_MOST, 2).astype(jnp.int32)
    lang_ids = set_ends(jax.random.randint(key_of[6], (SEGS,), 0, NLANG), jax.random.fold_in(key_of[6], 1), 0, NLANG - 1).astype(jnp.int32)
    return {"queries": queries, "keys": keys, "values": values, "out_weight": out_weight, "windows": windows, "seg_lengths": seg_lengths, "lang_ids": lang_ids}


def reference(queries, keys, values, out_weight, windows, seg_lengths, lang_ids):
    group = HEADS // KVH
    padded_keys = jnp.pad(keys, ((WINDOW, WINDOW), (0, 0)))
    padded_values = jnp.pad(values, ((WINDOW, WINDOW), (0, 0)))
    span = TOK_DEV + 2 * WINDOW
    head_windows = windows.reshape(KVH, group)

    def block(index):
        start = (index * TOK_DEV).astype(jnp.int32)
        query_block = lax.dynamic_slice_in_dim(queries, start, TOK_DEV, 0).astype(jnp.float32).reshape(TOK_DEV, KVH, group, HD)
        key_block = lax.dynamic_slice_in_dim(padded_keys, start, span, 0).astype(jnp.float32).reshape(span, KVH, HD)
        value_block = lax.dynamic_slice_in_dim(padded_values, start, span, 0).astype(jnp.float32).reshape(span, KVH, HD)
        scores = jnp.einsum("tkgd,nkd->kgtn", query_block, key_block) * (HD ** -0.5)
        query_pos = start + jnp.arange(TOK_DEV, dtype=jnp.int32)
        key_pos = start - WINDOW + jnp.arange(span, dtype=jnp.int32)
        distance = jnp.abs(query_pos[:, None] - key_pos[None, :])
        inside = (key_pos >= 0) & (key_pos < LENGTH)
        allowed = (distance[None, None] <= head_windows[:, :, None, None]) & inside[None, None, None, :]
        scores = jnp.where(allowed, scores, jnp.float32(-1e30))
        top = jnp.max(scores, axis=-1, keepdims=True)
        probs = jnp.where(allowed, jnp.exp(scores - top), jnp.float32(0.0))
        denom = jnp.sum(probs, axis=-1)
        rounded = lax.optimization_barrier(probs.astype(jnp.bfloat16)).astype(jnp.float32)
        mixed = jnp.einsum("kgtn,nkd->kgtd", rounded, value_block) / denom[..., None]
        return mixed.transpose(2, 0, 1, 3).reshape(TOK_DEV, HEADS * HD).astype(jnp.bfloat16)

    attn = lax.map(block, jnp.arange(N_SEQ, dtype=jnp.int32)).reshape(LENGTH, HEADS * HD)
    tokens = jnp.dot(attn, out_weight, preferred_element_type=jnp.float32)
    ends = jnp.cumsum(seg_lengths).astype(jnp.int32)
    starts = ends - seg_lengths
    positions = jnp.arange(LENGTH, dtype=jnp.int32)
    seg_hot = ((positions[:, None] >= starts[None, :]) & (positions[:, None] < ends[None, :])).astype(jnp.float32)
    span_sum = jnp.dot(seg_hot.T, tokens, precision=lax.Precision.HIGHEST)
    lang_hot = (lang_ids[:, None] == jnp.arange(NLANG, dtype=jnp.int32)[None, :]).astype(jnp.float32)
    lang_sum = jnp.dot(lang_hot.T, span_sum, precision=lax.Precision.HIGHEST)
    lang_count = jnp.sum(lang_hot * seg_lengths.astype(jnp.float32)[:, None], axis=0)
    lang_mean = lang_sum / jnp.maximum(lang_count, 1.0)[:, None]
    seg_center = jnp.dot(lang_hot, lang_mean, precision=lax.Precision.HIGHEST)
    centered = (tokens - jnp.dot(seg_hot, seg_center, precision=lax.Precision.HIGHEST)).astype(jnp.bfloat16)
    pooled = span_sum / seg_lengths.astype(jnp.float32)[:, None] - seg_center
    return centered, pooled
```

```python
import functools

import jax
import jax.numpy as jnp
from jax import lax
from jax.experimental import pallas as pl
from jax.experimental.pallas import tpu as pltpu
from jax.sharding import PartitionSpec as P

HD = 128
NEG = -1e30
LOG2E = 1.4426950408889634


def remote(src, dst, send, recv, device):
    return pltpu.make_async_remote_copy(
        src_ref=src,
        dst_ref=dst,
        send_sem=send,
        recv_sem=recv,
        device_id=device,
        device_id_type=pl.DeviceIdType.MESH,
    )


def each(low, high, body):
    if high - low <= 8:
        for i in range(low, high):
            body(i)
    else:

        def step(i, carry):
            body(i)
            return carry

        lax.fori_loop(low, high, step, 0)


def pack(x):
    half = x.shape[1] // 2
    return jnp.concatenate([x[:, :half], x[:, half:]], axis=0)


def unpack(x):
    rows = x.shape[0] // 2
    return jnp.concatenate([x[:rows], x[rows:]], axis=1)


def dot(a, b, dims=((1,), (0,))):
    return lax.dot_general(a, b, (dims, ((), ())), preferred_element_type=jnp.float32)


def kernel(
    n, heads, reach, owners,
    q_ref, k_ref, v_ref, win_ref, len_ref, lang_ref, w_ref,
    cent_ref, pool_ref,
    kbuf, vbuf, qs, m_s, l_s, acc, attn, wbuf, pout, pin, xout, xin, toks,
    sp_out, sp_in, hs_out, hs_in, sf, hot_t, hot, same_s, cnt_s, len_s,
    kv_send, kv_recv, w_sem, p_send, p_recv, x_send, x_recv,
    s1_send, s1_recv, h_send, h_recv, s2_send, s2_recv,
):
    p = lax.axis_index("seq")
    hd_me = lax.axis_index("head")
    nx = heads // 2
    x, c = hd_me // 2, hd_me % 2
    tok = q_ref.shape[0]
    kv_heads = k_ref.shape[1] // HD
    group = q_ref.shape[1] // k_ref.shape[1]
    lanes = group * tok
    segs = len_ref.shape[1]
    radius = reach // 2
    pair, par = p // 2, p % 2
    chunks, jc = wbuf.shape[2], wbuf.shape[4]
    cols = chunks * jc
    stride = n // owners
    rows = segs // owners

    barrier = pltpu.get_barrier_semaphore()

    def greet_seq(i):
        pl.semaphore_signal(
            barrier, inc=1, device_id={"seq": (p + i) % n}, device_id_type=pl.DeviceIdType.MESH
        )

    each(1, n, greet_seq)
    for i in range(1, heads):
        pl.semaphore_signal(
            barrier,
            inc=1,
            device_id={"head": (hd_me + i) % heads},
            device_id_type=pl.DeviceIdType.MESH,
        )

    def w_copy(k, cc, j):
        side = c if cc else 1 - c
        off = (((x + k) % nx) * 2 + side) * cols + j * jc
        return pltpu.make_async_copy(
            w_ref.at[:, pl.ds(pl.multiple_of(off, 128), jc)], wbuf.at[k, cc, j], w_sem.at[k, cc, j]
        )

    x_order = list(range(1, nx)) + [0]
    pl.semaphore_wait(barrier, n - 1 + heads - 1)

    offsets = [s * d for d in range(1, reach + 1) for s in (1, -1)]

    def kv_copy(i, o, which):
        d = p + o
        r = pair - d // 2 + radius
        src, buf = ((k_ref, kbuf), (v_ref, vbuf))[which]
        return remote(
            src, buf.at[r, par], kv_send.at[i, which], kv_recv.at[r, par, which], {"seq": d}
        )

    for i, o in enumerate(offsets):

        @pl.when((p + o >= 0) & (p + o < n))
        def _():
            kv_copy(i, o, 0).start()
            kv_copy(i, o, 1).start()

    for k in x_order:
        for cc in range(2):
            for j in range(chunks):
                w_copy(k, cc, j).start()

    kbuf[radius, par] = k_ref[...]
    vbuf[radius, par] = v_ref[...]
    for g in range(kv_heads):
        for h in range(group):
            at = (g * group + h) * HD
            qs[g, h * tok : (h + 1) * tok, :] = q_ref[:, at : at + HD]

    i0 = lax.broadcasted_iota(jnp.int32, (segs, segs), 0)
    i1 = lax.broadcasted_iota(jnp.int32, (segs, segs), 1)
    len_row = len_ref[...].astype(jnp.float32)
    lang_row = lang_ref[...].astype(jnp.float32)
    len_b = jnp.broadcast_to(len_row, (segs, segs))
    lang_b = jnp.broadcast_to(lang_row, (segs, segs))
    ends_col = jnp.sum(jnp.where(i1 <= i0, len_b, 0.0), axis=1, keepdims=True)
    len_col = jnp.sum(jnp.where(i1 == i0, len_b, 0.0), axis=1, keepdims=True)
    lang_col = jnp.sum(jnp.where(i1 == i0, lang_b, 0.0), axis=1, keepdims=True)
    len_cb = jnp.broadcast_to(len_col, (segs, segs))
    ends_row = jnp.sum(jnp.where(i0 <= i1, len_cb, 0.0), axis=0, keepdims=True)
    same = lang_b == jnp.broadcast_to(lang_col, (segs, segs))
    cnt_s[...] = jnp.maximum(jnp.sum(jnp.where(same, len_b, 0.0), axis=1, keepdims=True), 1.0)
    len_s[...] = len_col
    same_s[...] = jnp.where(same, 1.0, 0.0).astype(jnp.bfloat16)
    pos_t = (lax.broadcasted_iota(jnp.int32, (segs, tok), 1) + p * tok).astype(jnp.float32)
    in_t = (pos_t >= ends_col - len_col) & (pos_t < ends_col)
    hot_t[...] = jnp.where(in_t, 1.0, 0.0).astype(jnp.bfloat16)
    pos = (lax.broadcasted_iota(jnp.int32, (tok, segs), 0) + p * tok).astype(jnp.float32)
    in_s = (pos >= ends_row - len_row) & (pos < ends_row)
    hot[...] = jnp.where(in_s, 1.0, 0.0).astype(jnp.bfloat16)

    win_rows = []
    for g in range(kv_heads):
        parts = [
            jnp.full((1, tok), win_ref[hd_me * kv_heads * group + g * group + h], jnp.int32)
            for h in range(group)
        ]
        win_rows.append(jnp.concatenate(parts, axis=1))

    m_s[...] = jnp.full(m_s.shape, NEG, jnp.float32)
    l_s[...] = jnp.zeros(l_s.shape, jnp.float32)
    acc[...] = jnp.zeros(acc.shape, jnp.float32)
    scale = HD**-0.5 * LOG2E

    def absorb(t, carry):
        away = (t + 1) // 2
        there = jnp.where(t % 2 == 1, -away, away)
        r = radius + there

        @pl.when((pair + there >= 0) & (pair + there < n // 2))
        def _():
            for b in range(2):
                block = 2 * (pair + there) + b
                gap = jnp.abs(block - p)

                @pl.when((gap > 0) & (gap <= reach))
                def _():
                    for which, buf in enumerate((kbuf, vbuf)):
                        remote(
                            buf.at[r, b],
                            buf.at[r, b],
                            kv_send.at[0, which],
                            kv_recv.at[r, b, which],
                            {"seq": block},
                        ).wait_recv()

                @pl.when(gap > reach)
                def _():
                    kbuf[r, b] = jnp.zeros(kbuf.shape[2:], kbuf.dtype)
                    vbuf[r, b] = jnp.zeros(vbuf.shape[2:], vbuf.dtype)

            keys = kbuf[r].reshape(2 * tok, kv_heads * HD)
            vals = vbuf[r].reshape(2 * tok, kv_heads * HD)
            key_pos = lax.broadcasted_iota(jnp.int32, (2 * tok, tok), 0)
            query_pos = lax.broadcasted_iota(jnp.int32, (2 * tok, tok), 1)
            dist = jnp.abs(key_pos - query_pos + (2 * (pair + there) - p) * tok)
            dist = jnp.concatenate([dist] * group, axis=1)
            for g in range(kv_heads):
                kb = keys[:, g * HD : (g + 1) * HD]
                vb = vals[:, g * HD : (g + 1) * HD]
                s = dot(kb, qs[g], ((1,), (1,)))
                s = jnp.where(dist <= win_rows[g], s, NEG)
                m_old = m_s[g]
                m_new = jnp.maximum(m_old, jnp.max(s, axis=0, keepdims=True))
                alpha = jnp.exp2((m_old - m_new) * scale)
                prob = jnp.exp2((s - m_new) * scale)
                l_s[g] = l_s[g] * alpha + jnp.sum(prob, axis=0, keepdims=True)
                acc[g] = acc[g] * alpha + dot(vb, prob.astype(jnp.bfloat16), ((0,), (0,)))
                m_s[g] = m_new

        return carry

    lax.fori_loop(0, 2 * radius + 1, absorb, 0)

    for g in range(kv_heads):
        a = acc[g] / l_s[g]
        for h in range(group):
            at = (g * group + h) * HD
            attn[:, at : at + HD] = a[:, h * tok : (h + 1) * tok].T.astype(jnp.bfloat16)

    summed = dot(hot_t[...], attn[...])
    for o in range(owners):
        sp_out[o] = pack(summed[o * rows : (o + 1) * rows]).astype(jnp.bfloat16)
    mine = p // stride

    def is_owner(d, body):
        if stride == 1:
            body()
        else:
            pl.when(d % stride == 0)(body)

    def s1_copy(i):
        d = (p + i) % n
        return remote(
            sp_out.at[d // stride], sp_in.at[p], s1_send.at[i], s1_recv.at[p], {"seq": d}
        )

    each(1, n, lambda i: is_owner((p + i) % n, lambda: s1_copy(i).start()))

    partner = x * 2 + 1 - c

    def p_copy(k, j):
        return remote(
            pout.at[k, j], pin.at[k, j], p_send.at[k, j], p_recv.at[k, j], {"head": partner}
        )

    def x_copy(k, j):
        to = ((x + k) % nx) * 2 + c
        return remote(xout.at[k, j], xin.at[k, j], x_send.at[k, j], x_recv.at[k, j], {"head": to})

    for k in x_order:

        def for_partner(j, carry):
            w_copy(k, 0, j).wait()
            pout[k, j] = dot(attn[...], wbuf[k, 0, j]).astype(jnp.bfloat16)
            p_copy(k, j).start()
            return carry

        lax.fori_loop(0, chunks, for_partner, 0)

        def for_me(j, carry):
            w_copy(k, 1, j).wait()
            part = dot(attn[...], wbuf[k, 1, j])
            p_copy(k, j).wait_recv()
            part = part + pin[k, j].astype(jnp.float32)
            if k:
                xout[k, j] = part.astype(jnp.bfloat16)
                x_copy(k, j).start()
            else:
                toks[j] = part
            return carry

        lax.fori_loop(0, chunks, for_me, 0)

    def h_copy(k, cc):
        side = c if cc else 1 - c
        to = ((x + k) % nx) * 2 + side
        return remote(
            hs_out.at[k, cc], hs_in.at[k, cc], h_send.at[k, cc], h_recv.at[k, cc], {"head": to}
        )

    def s2_copy(i):
        return remote(sf.at[mine], sf.at[mine], s2_send.at[i], s2_recv.at[mine], {"seq": (p + i) % n})

    others = [(k, cc) for k in x_order for cc in range(2) if k or not cc]

    def own_spans():
        def take(i):
            d = (p + i) % n
            remote(
                sp_in.at[d], sp_in.at[d], s1_send.at[i], s1_recv.at[d], {"seq": d}
            ).wait_recv()

        each(1, n, take)
        sp_in[p] = sp_out[mine]
        total = unpack(jnp.sum(sp_in[...].astype(jnp.float32), axis=0))
        high = total.astype(jnp.bfloat16)
        low = (total - high.astype(jnp.float32)).astype(jnp.bfloat16)
        both = jnp.concatenate([high, low], axis=0)

        def through(k, cc):
            made = [dot(both, wbuf[k, cc, j]) for j in range(chunks)]
            return jnp.concatenate([y[:rows] + y[rows:] for y in made], axis=1)

        for k, cc in others:
            hs_out[k, cc] = pack(through(k, cc)).astype(jnp.bfloat16)
            h_copy(k, cc).start()
        result = pack(through(0, 1))
        for k, cc in others:
            h_copy(k, cc).wait_recv()
            result = result + hs_in[k, cc].astype(jnp.float32)
        sf[mine] = result.astype(jnp.bfloat16)
        each(1, n, lambda i: s2_copy(i).start())

    is_owner(p, own_spans)

    for j in range(chunks):
        for k in range(1, nx):
            x_copy(k, j).wait_recv()
            toks[j] = toks[j] + xin[k, j].astype(jnp.float32)

    def take_spans(i):
        d = (p + i) % n

        def take():
            o = d // stride
            remote(sf.at[o], sf.at[o], s2_send.at[i], s2_recv.at[o], {"seq": d}).wait_recv()

        is_owner(d, take)

    each(1, n, take_spans)

    spans = jnp.concatenate([unpack(sf[o]) for o in range(owners)], axis=0)
    center = dot(same_s[...], spans) / cnt_s[...]
    pool_ref[...] = spans.astype(jnp.float32) / len_s[...] - center
    high = center.astype(jnp.bfloat16)
    low = (center - high.astype(jnp.float32)).astype(jnp.bfloat16)
    moved = dot(hot[...], high) + dot(hot[...], low)
    for j in range(chunks):
        at = slice(j * jc, (j + 1) * jc)
        cent_ref[:, at] = (toks[j] - moved[:, at]).astype(jnp.bfloat16)

    for i, o in enumerate(offsets):

        @pl.when((p + o >= 0) & (p + o < n))
        def _():
            kv_copy(i, o, 0).wait_send()
            kv_copy(i, o, 1).wait_send()

    each(1, n, lambda i: is_owner((p + i) % n, lambda: s1_copy(i).wait_send()))
    for k in range(nx):
        for j in range(chunks):
            p_copy(k, j).wait_send()
            if k:
                x_copy(k, j).wait_send()

    def own_sends():
        for k, cc in others:
            h_copy(k, cc).wait_send()
        each(1, n, lambda i: s2_copy(i).wait_send())

    is_owner(p, own_sends)


def on_device(n, heads, queries, keys, values, out_weight, windows, seg_lengths, lang_ids):
    tok, q_cols = queries.shape
    kv_cols = keys.shape[1]
    kv_heads, group = kv_cols // HD, q_cols // kv_cols
    depth, width = out_weight.shape
    cols = width // heads
    segs = seg_lengths.shape[0]
    reach = min(16, n // 2)
    radius = reach // 2
    owners = min(n, segs // 8)
    rows = segs // owners
    nx = heads // 2
    chunks = 4
    jc = cols // chunks
    lanes = group * tok
    slots = 2 * radius + 1
    bf, f32 = jnp.bfloat16, jnp.float32
    packed = (2 * rows, cols // 2)
    packed_in = (2 * rows, q_cols // 2)
    dma = pltpu.SemaphoreType.DMA
    vmem = pl.BlockSpec(memory_space=pltpu.VMEM)
    return pl.pallas_call(
        functools.partial(kernel, n, heads, reach, owners),
        out_shape=(
            jax.ShapeDtypeStruct((tok, cols), bf),
            jax.ShapeDtypeStruct((segs, cols), f32),
        ),
        in_specs=[
            vmem,
            vmem,
            vmem,
            pl.BlockSpec(memory_space=pltpu.SMEM),
            vmem,
            vmem,
            pl.BlockSpec(memory_space=pl.ANY),
        ],
        out_specs=(vmem, vmem),
        scratch_shapes=[
            pltpu.VMEM((slots, 2, tok, kv_cols), bf),
            pltpu.VMEM((slots, 2, tok, kv_cols), bf),
            pltpu.VMEM((kv_heads, lanes, HD), bf),
            pltpu.VMEM((kv_heads, 1, lanes), f32),
            pltpu.VMEM((kv_heads, 1, lanes), f32),
            pltpu.VMEM((kv_heads, HD, lanes), f32),
            pltpu.VMEM((tok, q_cols), bf),
            pltpu.VMEM((nx, 2, chunks, depth, jc), bf),
            pltpu.VMEM((nx, chunks, tok, jc), bf),
            pltpu.VMEM((nx, chunks, tok, jc), bf),
            pltpu.VMEM((nx, chunks, tok, jc), bf),
            pltpu.VMEM((nx, chunks, tok, jc), bf),
            pltpu.VMEM((chunks, tok, jc), f32),
            pltpu.VMEM((owners,) + packed_in, bf),
            pltpu.VMEM((n,) + packed_in, bf),
            pltpu.VMEM((nx, 2) + packed, bf),
            pltpu.VMEM((nx, 2) + packed, bf),
            pltpu.VMEM((owners,) + packed, bf),
            pltpu.VMEM((segs, tok), bf),
            pltpu.VMEM((tok, segs), bf),
            pltpu.VMEM((segs, segs), bf),
            pltpu.VMEM((segs, 1), f32),
            pltpu.VMEM((segs, 1), f32),
            dma((2 * reach, 2)),
            dma((slots, 2, 2)),
            dma((nx, 2, chunks)),
            dma((nx, chunks)),
            dma((nx, chunks)),
            dma((nx, chunks)),
            dma((nx, chunks)),
            dma((n,)),
            dma((n,)),
            dma((nx, 2)),
            dma((nx, 2)),
            dma((n,)),
            dma((owners,)),
        ],
        compiler_params=pltpu.CompilerParams(
            collective_id=0, has_side_effects=True, vmem_limit_bytes=40 * 2**20
        ),
        cost_estimate=pl.CostEstimate(
            flops=2 * tok * depth * width, bytes_accessed=2 * depth * width, transcendentals=0
        ),
    )(
        queries,
        keys,
        values,
        windows,
        seg_lengths.reshape(1, segs),
        lang_ids.reshape(1, segs),
        out_weight,
    )


def solution(mesh):
    in_specs = (
        P("seq", "head"),
        P("seq", "head"),
        P("seq", "head"),
        P("head", None),
        P(),
        P(),
        P(),
    )
    out_specs = (P("seq", "head"), P(None, "head"))
    return jax.shard_map(
        functools.partial(on_device, mesh.shape["seq"], mesh.shape["head"]),
        mesh=mesh,
        in_specs=in_specs,
        out_specs=out_specs,
        check_vma=False,
    )
```

```python
import functools

import jax
import jax.numpy as jnp
from jax import lax
from jax.experimental import pallas as pl
from jax.experimental.pallas import tpu as pltpu
from jax.sharding import PartitionSpec as P

HD = 128
NEG = -1e30
LOG2E = 1.4426950408889634


def remote(src, dst, send, recv, device):
    return pltpu.make_async_remote_copy(
        src_ref=src,
        dst_ref=dst,
        send_sem=send,
        recv_sem=recv,
        device_id=device,
        device_id_type=pl.DeviceIdType.MESH,
    )


def each(low, high, body):
    if high - low <= 8:
        for i in range(low, high):
            body(i)
    else:

        def step(i, carry):
            body(i)
            return carry

        lax.fori_loop(low, high, step, 0)


def pack(x):
    half = x.shape[1] // 2
    return jnp.concatenate([x[:, :half], x[:, half:]], axis=0)


def unpack(x):
    rows = x.shape[0] // 2
    return jnp.concatenate([x[:rows], x[rows:]], axis=1)


def dot(a, b, dims=((1,), (0,))):
    return lax.dot_general(a, b, (dims, ((), ())), preferred_element_type=jnp.float32)


def kernel(
    n, heads, reach, owners,
    q_hbm, k_ref, v_ref, win_hbm, len_hbm, lang_hbm, w_ref,
    cent_ref, pool_ref,
    win_ref, len_ref, lang_ref, kbuf, vbuf, qs, m_s, l_s, acc, attn, wbuf, pout, pin, xout, xin, toks,
    sp_out, sp_in, hs_out, hs_in, sf, hot_t, hot, same_s, cnt_s, len_s,
    kv_send, kv_recv, w_sem, p_send, p_recv, x_send, x_recv,
    s1_send, s1_recv, h_send, h_recv, s2_send, s2_recv, in_sem, q_sem,
):
    p = lax.axis_index("seq")
    hd_me = lax.axis_index("head")
    nx = heads // 2
    x, c = hd_me // 2, hd_me % 2
    tok = q_hbm.shape[0]
    kv_heads = k_ref.shape[1] // HD
    group = q_hbm.shape[1] // k_ref.shape[1]
    segs = len_ref.shape[1]
    radius = reach // 2
    pair, par = p // 2, p % 2
    chunks, jc = wbuf.shape[2], wbuf.shape[4]
    cols = chunks * jc
    stride = n // owners
    rows = segs // owners

    barrier = pltpu.get_barrier_semaphore()

    def greet_seq(i):
        pl.semaphore_signal(
            barrier, inc=1, device_id={"seq": (p + i) % n}, device_id_type=pl.DeviceIdType.MESH
        )

    each(1, n, greet_seq)
    for i in range(1, heads):
        pl.semaphore_signal(
            barrier,
            inc=1,
            device_id={"head": (hd_me + i) % heads},
            device_id_type=pl.DeviceIdType.MESH,
        )

    def w_copy(k, cc, j):
        side = c if cc else 1 - c
        off = (((x + k) % nx) * 2 + side) * cols + j * jc
        return pltpu.make_async_copy(
            w_ref.at[:, pl.ds(pl.multiple_of(off, 128), jc)], wbuf.at[k, cc, j], w_sem.at[k, cc, j]
        )

    x_order = list(range(1, nx)) + [0]
    small = [
        pltpu.make_async_copy(src, dst, in_sem.at[i])
        for i, (src, dst) in enumerate(
            (
                (len_hbm, len_ref),
                (lang_hbm, lang_ref),
                (win_hbm, win_ref),
                (k_ref, kbuf.at[radius, par]),
                (v_ref, vbuf.at[radius, par]),
            )
        )
    ]
    for g in range(kv_heads):
        for h in range(group):
            at = (g * group + h) * HD
            small.append(
                pltpu.make_async_copy(
                    q_hbm.at[:, at : at + HD],
                    qs.at[g, h * tok : (h + 1) * tok, :],
                    q_sem.at[g, h],
                )
            )
    for copy in small:
        copy.start()
    pl.semaphore_wait(barrier, n - 1 + heads - 1)

    offsets = [s * d for d in range(1, reach + 1) for s in (1, -1)]

    def kv_copy(i, o, which):
        d = p + o
        r = pair - d // 2 + radius
        src, buf = ((k_ref, kbuf), (v_ref, vbuf))[which]
        return remote(
            src, buf.at[r, par], kv_send.at[i, which], kv_recv.at[r, par, which], {"seq": d}
        )

    for i, o in enumerate(offsets):

        @pl.when((p + o >= 0) & (p + o < n))
        def _():
            kv_copy(i, o, 0).start()
            kv_copy(i, o, 1).start()

    for k in x_order:
        for cc in range(2):
            for j in range(chunks):
                w_copy(k, cc, j).start()

    for copy in small:
        copy.wait()

    i0 = lax.broadcasted_iota(jnp.int32, (segs, segs), 0)
    i1 = lax.broadcasted_iota(jnp.int32, (segs, segs), 1)
    len_row = len_ref[...].astype(jnp.float32)
    lang_row = lang_ref[...].astype(jnp.float32)
    len_b = jnp.broadcast_to(len_row, (segs, segs))
    lang_b = jnp.broadcast_to(lang_row, (segs, segs))
    ends_col = jnp.sum(jnp.where(i1 <= i0, len_b, 0.0), axis=1, keepdims=True)
    len_col = jnp.sum(jnp.where(i1 == i0, len_b, 0.0), axis=1, keepdims=True)
    lang_col = jnp.sum(jnp.where(i1 == i0, lang_b, 0.0), axis=1, keepdims=True)
    len_cb = jnp.broadcast_to(len_col, (segs, segs))
    ends_row = jnp.sum(jnp.where(i0 <= i1, len_cb, 0.0), axis=0, keepdims=True)
    same = lang_b == jnp.broadcast_to(lang_col, (segs, segs))
    cnt_s[...] = jnp.maximum(jnp.sum(jnp.where(same, len_b, 0.0), axis=1, keepdims=True), 1.0)
    len_s[...] = len_col
    same_s[...] = jnp.where(same, 1.0, 0.0).astype(jnp.bfloat16)
    pos_t = (lax.broadcasted_iota(jnp.int32, (segs, tok), 1) + p * tok).astype(jnp.float32)
    in_t = (pos_t >= ends_col - len_col) & (pos_t < ends_col)
    hot_t[...] = jnp.where(in_t, 1.0, 0.0).astype(jnp.bfloat16)
    pos = (lax.broadcasted_iota(jnp.int32, (tok, segs), 0) + p * tok).astype(jnp.float32)
    in_s = (pos >= ends_row - len_row) & (pos < ends_row)
    hot[...] = jnp.where(in_s, 1.0, 0.0).astype(jnp.bfloat16)

    win_rows = []
    for g in range(kv_heads):
        parts = [
            jnp.full((1, tok), win_ref[hd_me * kv_heads * group + g * group + h], jnp.int32)
            for h in range(group)
        ]
        win_rows.append(jnp.concatenate(parts, axis=1))

    m_s[...] = jnp.full(m_s.shape, NEG, jnp.float32)
    l_s[...] = jnp.zeros(l_s.shape, jnp.float32)
    acc[...] = jnp.zeros(acc.shape, jnp.float32)
    scale = HD**-0.5 * LOG2E

    def absorb(t, carry):
        away = (t + 1) // 2
        there = jnp.where(t % 2 == 1, -away, away)
        r = radius + there

        @pl.when((pair + there >= 0) & (pair + there < n // 2))
        def _():
            for b in range(2):
                block = 2 * (pair + there) + b
                gap = jnp.abs(block - p)

                @pl.when((gap > 0) & (gap <= reach))
                def _():
                    for which, buf in enumerate((kbuf, vbuf)):
                        remote(
                            buf.at[r, b],
                            buf.at[r, b],
                            kv_send.at[0, which],
                            kv_recv.at[r, b, which],
                            {"seq": block},
                        ).wait_recv()

                @pl.when(gap > reach)
                def _():
                    kbuf[r, b] = jnp.zeros(kbuf.shape[2:], kbuf.dtype)
                    vbuf[r, b] = jnp.zeros(vbuf.shape[2:], vbuf.dtype)

            keys = kbuf[r].reshape(2 * tok, kv_heads * HD)
            vals = vbuf[r].reshape(2 * tok, kv_heads * HD)
            key_pos = lax.broadcasted_iota(jnp.int32, (2 * tok, tok), 0)
            query_pos = lax.broadcasted_iota(jnp.int32, (2 * tok, tok), 1)
            dist = jnp.abs(key_pos - query_pos + (2 * (pair + there) - p) * tok)
            dist = jnp.concatenate([dist] * group, axis=1)
            for g in range(kv_heads):
                kb = keys[:, g * HD : (g + 1) * HD]
                vb = vals[:, g * HD : (g + 1) * HD]
                s = dot(kb, qs[g], ((1,), (1,)))
                s = jnp.where(dist <= win_rows[g], s, NEG)
                m_old = m_s[g]
                m_new = jnp.maximum(m_old, jnp.max(s, axis=0, keepdims=True))
                alpha = jnp.exp2((m_old - m_new) * scale)
                prob = jnp.exp2((s - m_new) * scale)
                l_s[g] = l_s[g] * alpha + jnp.sum(prob, axis=0, keepdims=True)
                acc[g] = acc[g] * alpha + dot(vb, prob.astype(jnp.bfloat16), ((0,), (0,)))
                m_s[g] = m_new

        return carry

    lax.fori_loop(0, 2 * radius + 1, absorb, 0)

    for g in range(kv_heads):
        a = acc[g] / l_s[g]
        for h in range(group):
            at = (g * group + h) * HD
            attn[:, at : at + HD] = a[:, h * tok : (h + 1) * tok].T.astype(jnp.bfloat16)

    summed = dot(hot_t[...], attn[...])
    for o in range(owners):
        sp_out[o] = pack(summed[o * rows : (o + 1) * rows]).astype(jnp.bfloat16)
    mine = p // stride

    def is_owner(d, body):
        if stride == 1:
            body()
        else:
            pl.when(d % stride == 0)(body)

    def s1_copy(i):
        d = (p + i) % n
        return remote(
            sp_out.at[d // stride], sp_in.at[p], s1_send.at[i], s1_recv.at[p], {"seq": d}
        )

    each(1, n, lambda i: is_owner((p + i) % n, lambda: s1_copy(i).start()))

    partner = x * 2 + 1 - c

    def p_copy(k, j):
        return remote(
            pout.at[k, j], pin.at[k, j], p_send.at[k, j], p_recv.at[k, j], {"head": partner}
        )

    def x_copy(k, j):
        to = ((x + k) % nx) * 2 + c
        return remote(xout.at[k, j], xin.at[k, j], x_send.at[k, j], x_recv.at[k, j], {"head": to})

    for k in x_order:

        def for_partner(j, carry):
            w_copy(k, 0, j).wait()
            pout[k, j] = dot(attn[...], wbuf[k, 0, j]).astype(jnp.bfloat16)
            p_copy(k, j).start()
            return carry

        lax.fori_loop(0, chunks, for_partner, 0)

        def for_me(j, carry):
            w_copy(k, 1, j).wait()
            part = dot(attn[...], wbuf[k, 1, j])
            p_copy(k, j).wait_recv()
            part = part + pin[k, j].astype(jnp.float32)
            if k:
                xout[k, j] = part.astype(jnp.bfloat16)
                x_copy(k, j).start()
            else:
                toks[j] = part
            return carry

        lax.fori_loop(0, chunks, for_me, 0)

    def h_copy(k, cc):
        side = c if cc else 1 - c
        to = ((x + k) % nx) * 2 + side
        return remote(
            hs_out.at[k, cc], hs_in.at[k, cc], h_send.at[k, cc], h_recv.at[k, cc], {"head": to}
        )

    def s2_copy(i):
        return remote(sf.at[mine], sf.at[mine], s2_send.at[i], s2_recv.at[mine], {"seq": (p + i) % n})

    others = [(k, cc) for k in x_order for cc in range(2) if k or not cc]

    def own_spans():
        def take(i):
            d = (p + i) % n
            remote(
                sp_in.at[d], sp_in.at[d], s1_send.at[i], s1_recv.at[d], {"seq": d}
            ).wait_recv()

        each(1, n, take)
        sp_in[p] = sp_out[mine]
        total = unpack(jnp.sum(sp_in[...].astype(jnp.float32), axis=0))
        high = total.astype(jnp.bfloat16)
        low = (total - high.astype(jnp.float32)).astype(jnp.bfloat16)
        both = jnp.concatenate([high, low], axis=0)

        def through(k, cc):
            made = [dot(both, wbuf[k, cc, j]) for j in range(chunks)]
            return jnp.concatenate([y[:rows] + y[rows:] for y in made], axis=1)

        for k, cc in others:
            hs_out[k, cc] = pack(through(k, cc)).astype(jnp.bfloat16)
            h_copy(k, cc).start()
        result = pack(through(0, 1))
        for k, cc in others:
            h_copy(k, cc).wait_recv()
            result = result + hs_in[k, cc].astype(jnp.float32)
        sf[mine] = result.astype(jnp.bfloat16)
        each(1, n, lambda i: s2_copy(i).start())

    is_owner(p, own_spans)

    for j in range(chunks):
        for k in range(1, nx):
            x_copy(k, j).wait_recv()
            toks[j] = toks[j] + xin[k, j].astype(jnp.float32)

    def take_spans(i):
        d = (p + i) % n

        def take():
            o = d // stride
            remote(sf.at[o], sf.at[o], s2_send.at[i], s2_recv.at[o], {"seq": d}).wait_recv()

        is_owner(d, take)

    each(1, n, take_spans)

    spans = jnp.concatenate([unpack(sf[o]) for o in range(owners)], axis=0)
    center = dot(same_s[...], spans) / cnt_s[...]
    pool_ref[...] = spans.astype(jnp.float32) / len_s[...] - center
    high = center.astype(jnp.bfloat16)
    low = (center - high.astype(jnp.float32)).astype(jnp.bfloat16)
    moved = dot(hot[...], high) + dot(hot[...], low)
    for j in range(chunks):
        at = slice(j * jc, (j + 1) * jc)
        cent_ref[:, at] = (toks[j] - moved[:, at]).astype(jnp.bfloat16)

    for i, o in enumerate(offsets):

        @pl.when((p + o >= 0) & (p + o < n))
        def _():
            kv_copy(i, o, 0).wait_send()
            kv_copy(i, o, 1).wait_send()

    each(1, n, lambda i: is_owner((p + i) % n, lambda: s1_copy(i).wait_send()))
    for k in range(nx):
        for j in range(chunks):
            p_copy(k, j).wait_send()
            if k:
                x_copy(k, j).wait_send()

    def own_sends():
        for k, cc in others:
            h_copy(k, cc).wait_send()
        each(1, n, lambda i: s2_copy(i).wait_send())

    is_owner(p, own_sends)


def on_device(n, heads, queries, keys, values, out_weight, windows, seg_lengths, lang_ids):
    tok, q_cols = queries.shape
    kv_cols = keys.shape[1]
    kv_heads, group = kv_cols // HD, q_cols // kv_cols
    depth, width = out_weight.shape
    cols = width // heads
    segs = seg_lengths.shape[0]
    reach = min(16, n // 2)
    radius = reach // 2
    owners = min(n, segs // 8)
    rows = segs // owners
    nx = heads // 2
    chunks = 4
    jc = cols // chunks
    lanes = group * tok
    slots = 2 * radius + 1
    bf, f32 = jnp.bfloat16, jnp.float32
    packed = (2 * rows, cols // 2)
    packed_in = (2 * rows, q_cols // 2)
    dma = pltpu.SemaphoreType.DMA
    vmem = pl.BlockSpec(memory_space=pltpu.VMEM)
    return pl.pallas_call(
        functools.partial(kernel, n, heads, reach, owners),
        out_shape=(
            jax.ShapeDtypeStruct((tok, cols), bf),
            jax.ShapeDtypeStruct((segs, cols), f32),
        ),
        in_specs=[pl.BlockSpec(memory_space=pl.ANY)] * 7,
        out_specs=(vmem, vmem),
        scratch_shapes=[
            pltpu.SMEM(windows.shape, jnp.int32),
            pltpu.VMEM((1, segs), jnp.int32),
            pltpu.VMEM((1, segs), jnp.int32),
            pltpu.VMEM((slots, 2, tok, kv_cols), bf),
            pltpu.VMEM((slots, 2, tok, kv_cols), bf),
            pltpu.VMEM((kv_heads, lanes, HD), bf),
            pltpu.VMEM((kv_heads, 1, lanes), f32),
            pltpu.VMEM((kv_heads, 1, lanes), f32),
            pltpu.VMEM((kv_heads, HD, lanes), f32),
            pltpu.VMEM((tok, q_cols), bf),
            pltpu.VMEM((nx, 2, chunks, depth, jc), bf),
            pltpu.VMEM((nx, chunks, tok, jc), bf),
            pltpu.VMEM((nx, chunks, tok, jc), bf),
            pltpu.VMEM((nx, chunks, tok, jc), bf),
            pltpu.VMEM((nx, chunks, tok, jc), bf),
            pltpu.VMEM((chunks, tok, jc), f32),
            pltpu.VMEM((owners,) + packed_in, bf),
            pltpu.VMEM((n,) + packed_in, bf),
            pltpu.VMEM((nx, 2) + packed, bf),
            pltpu.VMEM((nx, 2) + packed, bf),
            pltpu.VMEM((owners,) + packed, bf),
            pltpu.VMEM((segs, tok), bf),
            pltpu.VMEM((tok, segs), bf),
            pltpu.VMEM((segs, segs), bf),
            pltpu.VMEM((segs, 1), f32),
            pltpu.VMEM((segs, 1), f32),
            dma((2 * reach, 2)),
            dma((slots, 2, 2)),
            dma((nx, 2, chunks)),
            dma((nx, chunks)),
            dma((nx, chunks)),
            dma((nx, chunks)),
            dma((nx, chunks)),
            dma((n,)),
            dma((n,)),
            dma((nx, 2)),
            dma((nx, 2)),
            dma((n,)),
            dma((owners,)),
            dma((5,)),
            dma((kv_heads, group)),
        ],
        compiler_params=pltpu.CompilerParams(
            collective_id=0, has_side_effects=True, vmem_limit_bytes=57 * 2**20
        ),
        cost_estimate=pl.CostEstimate(
            flops=2 * tok * depth * width, bytes_accessed=2 * depth * width, transcendentals=0
        ),
    )(
        queries,
        keys,
        values,
        windows,
        seg_lengths.reshape(1, segs),
        lang_ids.reshape(1, segs),
        out_weight,
    )


def solution(mesh):
    in_specs = (
        P("seq", "head"),
        P("seq", "head"),
        P("seq", "head"),
        P("head", None),
        P(),
        P(),
        P(),
    )
    out_specs = (P("seq", "head"), P(None, "head"))
    return jax.shard_map(
        functools.partial(on_device, mesh.shape["seq"], mesh.shape["head"]),
        mesh=mesh,
        in_specs=in_specs,
        out_specs=out_specs,
        check_vma=False,
    )
```
